32 devices in a mesh: row: 16 (over z, y, x), col: 2 (over core).
Axes of the slice: x: 2, y: 2, z: 4, core: 2. Of those that a mesh axis runs over, the one named last changes fastest.
Arguments:
- factor: bfloat16 [2, 2048, 65536], P(None, 'row', 'col'), may hold values from -40 to 40
- scales: float32 [2, 16, 512], P(None, 'row', 'col'), may hold values from 0 to 1, as said below
- coords: float32 [2, 2, 2048], replicated, may hold values from 0 to 1
- jitter: float32 [1], replicated, may hold values from 1 to 2
Outputs:
- new_columns: float32 [2, 2048, 256], P(None, ('row', 'col'))
The draws below stay inside these ranges and needn't reach their ends.
Inputs may be any that keep to these rules, and one draw needn't show every extreme that they name: `scales`: positive.
All inputs are finite; a program needn't handle non-finite values.
Results may differ from the reference program's by a relative error of at most 0.0003.
Values may be sent and summed in bfloat16 or wider, within the bound.
A program may use at most 192 MiB of HBM per device.

```python
import math
import jax
import jax.numpy as jnp
from jax import lax

PANEL = 128
CYC = 2
KF = 65536
KB = 512
N_ROW = 16


def draw_factor(key, part):
    key_lead = jax.random.fold_in(key, 11)
    key_mix = jax.random.fold_in(key, 12)
    leading = jnp.clip(jax.random.normal(key_lead, (2 * PANEL, KF), jnp.float32), -4.0, 4.0)

    def one_block(index):
        block_key = jax.random.fold_in(key_mix, index)
        key_one, key_two = jax.random.split(block_key, 2)
        mixing = 0.5 * jax.random.normal(key_one, (PANEL, 2 * PANEL), jnp.float32)
        noise = jax.random.normal(key_two, (PANEL, KF), jnp.float32)
        mixed = jnp.clip(jnp.dot(mixing, leading) + noise, -40.0, 40.0)
        own_rows = lax.dynamic_slice_in_dim(leading, jnp.minimum(index, 1) * PANEL, PANEL, 0)
        return jnp.where(index < 2, own_rows, mixed).astype(jnp.bfloat16)
    stacked = lax.map(one_block, jnp.arange(CYC * N_ROW, dtype=jnp.int32))
    return stacked.reshape(CYC, N_ROW * PANEL, KF)


def draw_scales(key, part):
    level = jax.random.uniform(jax.random.fold_in(key, 21), (CYC, N_ROW, KB), jnp.float32, math.log(0.3), math.log(3.0))
    return jnp.exp(level) * (0.25 / math.sqrt(KF))


def setup_inputs(seed: int = 0) -> dict:
    seeds = jax.random.split(jax.random.key(seed), 5)
    return {
        "factor": draw_factor(jax.random.fold_in(seeds[4], 71), 0),
        "scales": draw_scales(jax.random.fold_in(seeds[4], 71), 0),
        "coords": jnp.clip(jax.random.uniform(seeds[2], (2, CYC, N_ROW * PANEL), jnp.float32, 0.0, 1.0), 0.0, 1.0),
        "jitter": jnp.clip(jax.random.uniform(seeds[3], (1,), jnp.float32, 1.0, 2.0), 1.0, 2.0),
    }


SQRT_THREE = 1.7320508075688772
LENGTH_SCALE = 0.25

def matern(left_pts, right_pts):
    diff_x = left_pts[0][:, None] - right_pts[0][None, :]
    diff_y = left_pts[1][:, None] - right_pts[1][None, :]
    scaled = SQRT_THREE * jnp.sqrt(diff_x * diff_x + diff_y * diff_y) / LENGTH_SCALE
    return (1.0 + scaled) * jnp.exp(-scaled)

def dequantize(block, scale_row):
    widened = block.astype(jnp.float32).reshape(PANEL, KB, PANEL) * scale_row[None, :, None]
    return widened.reshape(PANEL, KF).astype(jnp.bfloat16)

def reference(factor, scales, coords, jitter):
    lead_width = 2 * PANEL
    block_count = CYC * N_ROW
    blocks = factor.reshape(block_count, PANEL, KF)
    block_scales = scales.reshape(block_count, KB)
    leading = jnp.concatenate([dequantize(blocks[0], block_scales[0]), dequantize(blocks[1], block_scales[1])], axis=0)

    def one_block(inputs):
        return lax.dot_general(dequantize(inputs[0], inputs[1]).astype(jnp.float32), leading.astype(jnp.float32), (((1,), (1,)), ((), ())), preferred_element_type=jnp.float32)
    products = lax.map(one_block, (blocks, block_scales)).reshape(block_count * PANEL, lead_width)
    points = coords.reshape(2, block_count * PANEL)
    lead_pts = points[:, :lead_width]
    rows_all = jnp.arange(block_count * PANEL, dtype=jnp.int32)
    identity_mask = (rows_all[:, None] == jnp.arange(lead_width, dtype=jnp.int32)[None, :]).astype(jnp.float32)
    window = matern(points, lead_pts) + jitter[0] * identity_mask - products
    factor_low = jnp.linalg.cholesky(window[:lead_width])
    result = jax.scipy.linalg.solve_triangular(factor_low, window.T, lower=True).T
    return result.reshape(CYC, N_ROW * PANEL, lead_width)
```

```python
import functools
import jax
import jax.numpy as jnp
from jax import lax
from jax.experimental import pallas as pl
from jax.experimental.pallas import tpu as pltpu
from jax.sharding import PartitionSpec as P

PANEL = 128
CHUNK = 256
SKEW = 2
HEAD = 8

SQRT_THREE = 1.7320508075688772
LENGTH_SCALE = 0.25
MESH = pl.DeviceIdType.MESH
TREES = 3
TWIN, CHAIN, LIFT = 0, 2, 1


def matern(left_pts, right_pts):
    diff_x = left_pts[0][:, None] - right_pts[0][None, :]
    diff_y = left_pts[1][:, None] - right_pts[1][None, :]
    scaled = SQRT_THREE * jnp.sqrt(diff_x * diff_x + diff_y * diff_y) / LENGTH_SCALE
    return (1.0 + scaled) * jnp.exp(-scaled)


def right_solve(factor_low, values):
    return jax.scipy.linalg.solve_triangular(factor_low, values.T, lower=True).T


def counts_of(chunks):
    return [chunks // TREES + (1 if t < chunks % TREES else 0) for t in range(TREES)]


def roles(tree, xs, y, z, planes):
    top = z == planes - 1
    low = z == 0
    a = (xs == 0) & (y == 0)
    b = (xs == 1) & (y == 0)
    c = (xs == 1) & (y == 1)
    d = (xs == 0) & (y == 1)
    up = jnp.logical_not(top)
    if tree == TWIN:
        return z + y + xs, xs == 0, a & low, (xs == 0) & up, None
    high = jnp.logical_not(low)
    if tree == CHAIN:
        place = jnp.where(d, 1, jnp.where(a, 2, jnp.where(b, 3, 4)))
        depth = jnp.where(low, xs + y, z + place)
        send_x = (low & (xs == 0)) | (high & a)
        send_y = (low & a) | (high & (d | b))
        return depth, send_x, send_y, d & up, None
    place = jnp.where(a, 0, jnp.where(d, 1, jnp.where(c, 2, 3)))
    depth = jnp.where(low, jnp.where(a, 0, place + 2), z + place)
    return depth, high & d, high & (a | c), a & up, (z == 1) & jnp.logical_not(a)


def gather_products(rows, factor_hbm, scales_ref, prod_ref, gram_ref,
                    raw, lead, lhs, acc, got_prod, got_gram,
                    load_sem, send_sem, recv_sem, swap_sem):
    cycles, _, width = raw.shape
    row = lax.axis_index("row")
    col = lax.axis_index("col")
    chunks = width // CHUNK
    counts = counts_of(chunks)
    starts = [sum(counts[:t]) for t in range(TREES)]
    planes = rows // 4
    x = row % 2
    y = (row // 2) % 2
    z = row // 4
    targets = [
        row + 1 - 2 * x,
        row + 2 - 4 * y,
        jnp.minimum(row + 4, rows - 1),
        jnp.maximum(row - 4, 0),
    ]
    has_up = z < planes - 1
    has_down = z > 0
    partner = 1 - col

    head = min(HEAD, min(counts) - 1)
    loads = []
    for t in range(TREES):
        for part, (low, size) in enumerate(((0, head), (head, counts[t] - head))):
            span = pl.ds((starts[t] + low) * CHUNK, size * CHUNK)
            loads.append(pltpu.make_async_copy(
                factor_hbm.at[:, :, span], raw.at[:, :, span], load_sem.at[t, part]))
    for t in range(TREES):
        loads[2 * t].start()
    for t in range(TREES):
        loads[2 * t + 1].start()

    barrier = pltpu.get_barrier_semaphore()

    def greet(target):
        pl.semaphore_signal(barrier, inc=1, device_id=target, device_id_type=MESH)

    greet((targets[0], col))
    greet((targets[1], col))
    greet((row, partner))
    pl.when(has_up)(lambda: greet((targets[2], col)))
    pl.when(has_down)(lambda: greet((targets[3], col)))
    acc[...] = jnp.zeros_like(acc)
    pl.semaphore_wait(barrier, 3 + has_up.astype(jnp.int32) + has_down.astype(jnp.int32))

    depths = [[None] * TREES for _ in range(2)]
    sends = [[None] * TREES for _ in range(2)]
    for s in range(2):
        xs = x if s == 0 else 1 - x
        for t in range(TREES):
            depth, *send = roles(t, xs, y, z, planes)
            depths[s][t] = depth
            sends[s][t] = send
    last = planes - 1 + 4

    def piece(s, t, index, size=1):
        return lead.at[s, :, pl.ds(pl.multiple_of((starts[t] + index) * CHUNK, CHUNK), size * CHUNK)]

    def dequantize(cycle, chunk, out, out_row, out_at):
        for b in range(CHUNK // PANEL):
            at = pl.multiple_of(chunk * CHUNK + b * PANEL, PANEL)
            scale = scales_ref[cycle, chunk * (CHUNK // PANEL) + b]
            block = raw[cycle, :, pl.ds(at, PANEL)].astype(jnp.float32) * scale
            out(b, block.astype(jnp.bfloat16))

    def forward(s, t, step):
        index = step - SKEW * depths[s][t]

        @pl.when((index >= 0) & (index < counts[t]))
        def _():
            here = piece(s, t, index)

            @pl.when(row == s)
            def _():
                def put(b, block):
                    at = pl.multiple_of((starts[t] + index) * CHUNK + b * PANEL, PANEL)
                    lead[s, :, pl.ds(at, PANEL)] = block
                dequantize(0, starts[t] + index, put, 0, 0)

            @pl.when(row != s)
            def _():
                pltpu.make_async_copy(here, here, recv_sem.at[s, t, index]).wait()

            for way in range(4):
                wanted = sends[s][t][way]
                if wanted is None:
                    continue

                @pl.when(wanted)
                def _():
                    pltpu.make_async_remote_copy(
                        src_ref=here, dst_ref=here,
                        send_sem=send_sem.at[s, t, way], recv_sem=recv_sem.at[s, t, index],
                        device_id=(targets[way], col), device_id_type=MESH,
                    ).start()

    def multiply(t, step):
        index = step - SKEW * jnp.maximum(depths[0][t], depths[1][t])

        @pl.when((index >= 0) & (index < counts[t]))
        def _():
            chunk = starts[t] + index
            for cycle in range(cycles):
                def put(b, block):
                    lhs[cycle * PANEL:(cycle + 1) * PANEL, b * PANEL:(b + 1) * PANEL] = block
                dequantize(cycle, chunk, put, 0, 0)
            span = pl.ds(pl.multiple_of(chunk * CHUNK, CHUNK), CHUNK)
            right = lead[:, :, span].reshape(2 * PANEL, CHUNK)
            own = lhs[...]
            dims = (((1,), (1,)), ((), ()))
            top = cycles * PANEL
            acc[:top] += lax.dot_general(own, right, dims, preferred_element_type=jnp.float32)
            acc[top:] += lax.dot_general(right, right, dims, preferred_element_type=jnp.float32)

    def one_step(step, carry):
        for t in range(TREES):
            for s in range(2):
                forward(s, t, step)
        for t in range(TREES):
            multiply(t, step)
        return carry

    for t in range(TREES):
        loads[2 * t].wait()
    lax.fori_loop(0, head, one_step, 0)
    for t in range(TREES):
        loads[2 * t + 1].wait()
    lax.fori_loop(head, max(counts) + SKEW * last, one_step, 0)

    share = PANEL // 2
    top = cycles * PANEL
    swaps = []
    for cycle in range(cycles):
        at = pl.multiple_of(cycle * PANEL + partner * share, share)
        swaps.append((acc.at[pl.ds(at, share)], got_prod.at[cycle]))
    swaps.append((acc.at[pl.ds(top, 2 * PANEL)], got_gram))
    copies = []
    for k, (source, target) in enumerate(swaps):
        copies.append(pltpu.make_async_remote_copy(
            src_ref=source, dst_ref=target, send_sem=swap_sem.at[0, k], recv_sem=swap_sem.at[1, k],
            device_id=(row, partner), device_id_type=MESH))
    for copy in copies:
        copy.start()
    for s in range(2):
        for t in range(TREES):
            for way in range(4):
                wanted = sends[s][t][way]
                if wanted is None:
                    continue

                @pl.when(wanted)
                def _():
                    whole = piece(s, t, 0, counts[t])
                    pltpu.make_async_remote_copy(
                        src_ref=whole, dst_ref=whole,
                        send_sem=send_sem.at[s, t, way], recv_sem=recv_sem.at[s, t, 0],
                        device_id=(targets[way], col), device_id_type=MESH,
                    ).wait_send()
    for copy in copies:
        copy.wait()
    for cycle in range(cycles):
        at = pl.multiple_of(cycle * PANEL + col * share, share)
        prod_ref[cycle] = acc[pl.ds(at, share)] + got_prod[cycle]
    gram_ref[...] = acc[top:] + got_gram[...]


def on_device(rows, factor, scales, coords, jitter):
    cycles, block_rows, width_local = factor.shape
    lead_width = 2 * PANEL
    col_count = lax.axis_size("col")
    share_rows = PANEL // col_count
    chunks = width_local // CHUNK
    pieces, gram_sum = pl.pallas_call(
        functools.partial(gather_products, rows),
        out_shape=(
            jax.ShapeDtypeStruct((cycles, share_rows, lead_width), jnp.float32),
            jax.ShapeDtypeStruct((lead_width, lead_width), jnp.float32),
        ),
        in_specs=[
            pl.BlockSpec(memory_space=pl.ANY),
            pl.BlockSpec(memory_space=pltpu.SMEM),
        ],
        out_specs=(
            pl.BlockSpec(memory_space=pltpu.VMEM),
            pl.BlockSpec(memory_space=pltpu.VMEM),
        ),
        scratch_shapes=[
            pltpu.VMEM((cycles, PANEL, width_local), jnp.bfloat16),
            pltpu.VMEM((2, PANEL, width_local), jnp.bfloat16),
            pltpu.VMEM((cycles * PANEL, CHUNK), jnp.bfloat16),
            pltpu.VMEM((cycles * PANEL + lead_width, lead_width), jnp.float32),
            pltpu.VMEM((cycles, share_rows, lead_width), jnp.float32),
            pltpu.VMEM((lead_width, lead_width), jnp.float32),
            pltpu.SemaphoreType.DMA((TREES, 2)),
            pltpu.SemaphoreType.DMA((2, TREES, 4)),
            pltpu.SemaphoreType.DMA((2, TREES, max(counts_of(chunks)))),
            pltpu.SemaphoreType.DMA((2, cycles + 1)),
        ],
        compiler_params=pltpu.CompilerParams(
            collective_id=0, has_side_effects=True, vmem_limit_bytes=48 * 1024 * 1024),
        cost_estimate=pl.CostEstimate(
            flops=8 * cycles * PANEL * lead_width * width_local,
            bytes_accessed=factor.size * 2, transcendentals=0),
        name="gather_products",
    )(factor, scales.reshape(cycles, -1))
    row_index = lax.axis_index("row")
    col_index = lax.axis_index("col")
    row_count = lax.axis_size("row")
    own_pts = lax.dynamic_slice_in_dim(
        coords, row_index * PANEL + col_index * share_rows, share_rows, 2
    ).reshape(2, cycles * share_rows)
    lead_pts = coords[:, 0, :lead_width]
    local_rows = jnp.arange(cycles * share_rows, dtype=jnp.int32)
    global_rows = (
        local_rows // share_rows * (row_count * PANEL)
        + row_index * PANEL + col_index * share_rows + local_rows % share_rows
    )
    identity_mask = (
        global_rows[:, None] == jnp.arange(lead_width, dtype=jnp.int32)[None, :]
    ).astype(jnp.float32)
    kernel = matern(own_pts, lead_pts) + jitter[0] * identity_mask
    lead_kernel = matern(lead_pts, lead_pts) + jitter[0] * jnp.eye(lead_width, dtype=jnp.float32)
    factor_low = jnp.linalg.cholesky(lead_kernel - gram_sum)
    window = kernel - pieces.reshape(cycles * share_rows, lead_width)
    return right_solve(factor_low, window).reshape(cycles, share_rows, lead_width)


def solution(mesh):
    placed = (P(None, "row", "col"), P(None, "row", "col"), P(), P())
    return jax.shard_map(
        functools.partial(on_device, mesh.shape["row"]),
        mesh=mesh,
        in_specs=placed,
        out_specs=P(None, ("row", "col"), None),
        check_vma=False,
    )
```

```python
import functools
import jax
import jax.numpy as jnp
from jax import lax
from jax.experimental import pallas as pl
from jax.experimental.pallas import tpu as pltpu
from jax.sharding import PartitionSpec as P

PANEL = 128
CHUNK = 128
PAIR = 2
SKEW = 2
HEAD = 16

SQRT_THREE = 1.7320508075688772
LENGTH_SCALE = 0.25
MESH = pl.DeviceIdType.MESH
TREES = 3
TWIN, CHAIN, LIFT = 0, 2, 1


def matern(left_pts, right_pts):
    diff_x = left_pts[0][:, None] - right_pts[0][None, :]
    diff_y = left_pts[1][:, None] - right_pts[1][None, :]
    scaled = SQRT_THREE * jnp.sqrt(diff_x * diff_x + diff_y * diff_y) / LENGTH_SCALE
    return (1.0 + scaled) * jnp.exp(-scaled)


def exact_dot(left, right, transposed):
    dims = (((1,), (1 if transposed else 0,)), ((), ()))
    return lax.dot_general(
        left, right, dims, precision=lax.Precision.HIGHEST, preferred_element_type=jnp.float32
    )


def inverse_factor(block, out_ref):
    size = block.shape[0]
    tiles = size // 8
    sub = lax.broadcasted_iota(jnp.int32, (8, size), 0)
    lane = lax.broadcasted_iota(jnp.int32, (8, size), 1)
    left = [block[8 * k:8 * k + 8] for k in range(tiles)]
    right = [(lane == sub + 8 * k).astype(jnp.float32) for k in range(tiles)]
    for j in range(size):
        home, r = j // 8, j % 8
        row_left = left[home][r:r + 1, :]
        row_right = right[home][r:r + 1, :]
        pivot = jnp.broadcast_to(row_left[:, j:j + 1], (1, size))
        out_ref[j:j + 1, :] = row_right * lax.rsqrt(pivot)
        if j == size - 1:
            break
        inverse = 1.0 / pivot
        scaled_left = row_left * inverse
        scaled_right = row_right * inverse
        for k in range(home, tiles):
            if k == home and r == 7:
                continue
            column = jnp.broadcast_to(left[k][:, j:j + 1], (8, size))
            if k == home:
                column = jnp.where(sub > r, column, 0.0)
            left[k] = left[k] - column * scaled_left
            right[k] = right[k] - column * scaled_right


def solve_panels(gram_ref, lead_ref, prod_ref, kernel_ref, out_ref, block, inv_one, inv_two):
    half = block.shape[0]
    block[...] = lead_ref[:half, :half] - gram_ref[:half, :half]
    inverse_factor(block[...], inv_one)
    first = inv_one[...]
    below = exact_dot(lead_ref[half:, :half] - gram_ref[half:, :half], first, True)
    block[...] = lead_ref[half:, half:] - gram_ref[half:, half:] - exact_dot(below, below, True)
    one = exact_dot(kernel_ref[:, :half] - prod_ref[:, :half], first, True)
    rest = kernel_ref[:, half:] - prod_ref[:, half:] - exact_dot(one, below, True)
    inverse_factor(block[...], inv_two)
    out_ref[:, :half] = one
    out_ref[:, half:] = exact_dot(rest, inv_two[...], True)


def counts_of(chunks):
    pairs = chunks // PAIR
    return [PAIR * (pairs // TREES + (1 if t < pairs % TREES else 0)) for t in range(TREES)]


def roles(tree, xs, y, z, planes):
    top = z == planes - 1
    low = z == 0
    a = (xs == 0) & (y == 0)
    b = (xs == 1) & (y == 0)
    c = (xs == 1) & (y == 1)
    d = (xs == 0) & (y == 1)
    up = jnp.logical_not(top)
    if tree == TWIN:
        return z + y + xs, xs == 0, a & low, (xs == 0) & up, None
    high = jnp.logical_not(low)
    if tree == CHAIN:
        place = jnp.where(d, 1, jnp.where(a, 2, jnp.where(b, 3, 4)))
        depth = jnp.where(low, xs + y, z + place)
        send_x = (low & (xs == 0)) | (high & a)
        send_y = (low & a) | (high & (d | b))
        return depth, send_x, send_y, d & up, None
    place = jnp.where(a, 0, jnp.where(d, 1, jnp.where(c, 2, 3)))
    depth = jnp.where(low, jnp.where(a, 0, place + 2), z + place)
    return depth, high & d, high & (a | c), a & up, (z == 1) & jnp.logical_not(a)


def gather_products(rows, factor_hbm, scales_ref, prod_ref, gram_ref,
                    raw, lead, lhs, acc, got_prod, got_gram,
                    load_sem, send_sem, recv_sem, swap_sem):
    cycles, _, width = raw.shape
    row = lax.axis_index("row")
    col = lax.axis_index("col")
    chunks = width // CHUNK
    counts = counts_of(chunks)
    starts = [sum(counts[:t]) for t in range(TREES)]
    planes = rows // 4
    x = row % 2
    y = (row // 2) % 2
    z = row // 4
    targets = [
        row + 1 - 2 * x,
        row + 2 - 4 * y,
        jnp.minimum(row + 4, rows - 1),
        jnp.maximum(row - 4, 0),
    ]
    has_up = z < planes - 1
    has_down = z > 0
    partner = 1 - col

    head = min(HEAD, min(counts) - PAIR)
    loads = []
    for t in range(TREES):
        for part, (low, size) in enumerate(((0, head), (head, counts[t] - head))):
            span = pl.ds((starts[t] + low) * CHUNK, size * CHUNK)
            loads.append(pltpu.make_async_copy(
                factor_hbm.at[:, :, span], raw.at[:, :, span], load_sem.at[t, part]))
    for t in range(TREES):
        loads[2 * t].start()
    for t in range(TREES):
        loads[2 * t + 1].start()

    barrier = pltpu.get_barrier_semaphore()

    def greet(target):
        pl.semaphore_signal(barrier, inc=1, device_id=target, device_id_type=MESH)

    greet((targets[0], col))
    greet((targets[1], col))
    greet((row, partner))
    pl.when(has_up)(lambda: greet((targets[2], col)))
    pl.when(has_down)(lambda: greet((targets[3], col)))
    acc[...] = jnp.zeros_like(acc)
    pl.semaphore_wait(barrier, 3 + has_up.astype(jnp.int32) + has_down.astype(jnp.int32))

    depths = [[None] * TREES for _ in range(2)]
    sends = [[None] * TREES for _ in range(2)]
    for s in range(2):
        xs = x if s == 0 else 1 - x
        for t in range(TREES):
            depth, *send = roles(t, xs, y, z, planes)
            depths[s][t] = depth
            sends[s][t] = send
    last = planes - 1 + 4

    def piece(s, t, index, size=1):
        return lead.at[s, pl.ds(starts[t] + index, size)]

    def dequantize(cycle, chunk):
        at = pl.multiple_of(chunk * CHUNK, CHUNK)
        block = raw[cycle, :, pl.ds(at, CHUNK)].astype(jnp.float32) * scales_ref[cycle, chunk]
        return block.astype(jnp.bfloat16)

    def forward(s, t, step):
        index = step - SKEW * depths[s][t]

        @pl.when((index >= 0) & (index < counts[t]))
        def _():
            here = piece(s, t, index)

            @pl.when(row == s)
            def _():
                lead[s, starts[t] + index] = dequantize(0, starts[t] + index)

            @pl.when(row != s)
            def _():
                pltpu.make_async_copy(here, here, recv_sem.at[s, t, index]).wait()

            for way in range(4):
                wanted = sends[s][t][way]
                if wanted is None:
                    continue

                @pl.when(wanted)
                def _():
                    pltpu.make_async_remote_copy(
                        src_ref=here, dst_ref=here,
                        send_sem=send_sem.at[s, t, way], recv_sem=recv_sem.at[s, t, index],
                        device_id=(targets[way], col), device_id_type=MESH,
                    ).start()

    def multiply(t, step):
        index = step - SKEW * jnp.maximum(depths[0][t], depths[1][t])

        @pl.when((index >= 0) & (index < counts[t]) & (index % PAIR == PAIR - 1))
        def _():
            first = starts[t] + index - (PAIR - 1)
            for cycle in range(cycles):
                for b in range(PAIR):
                    lhs[cycle * PANEL:(cycle + 1) * PANEL, b * CHUNK:(b + 1) * CHUNK] = (
                        dequantize(cycle, first + b))
            right = jnp.concatenate([
                jnp.concatenate([lead[s, first + b] for b in range(PAIR)], axis=1)
                for s in range(2)], axis=0)
            own = lhs[...]
            dims = (((1,), (1,)), ((), ()))
            top = cycles * PANEL
            acc[:top] += lax.dot_general(own, right, dims, preferred_element_type=jnp.float32)
            acc[top:] += lax.dot_general(right, right, dims, preferred_element_type=jnp.float32)

    def one_step(step, carry):
        for t in range(TREES):
            for s in range(2):
                forward(s, t, step)
        for t in range(TREES):
            multiply(t, step)
        return carry

    for t in range(TREES):
        loads[2 * t].wait()
    lax.fori_loop(0, head, one_step, 0)
    for t in range(TREES):
        loads[2 * t + 1].wait()
    lax.fori_loop(head, max(counts) + SKEW * last, one_step, 0)

    share = PANEL // 2
    top = cycles * PANEL
    swaps = []
    for cycle in range(cycles):
        at = pl.multiple_of(cycle * PANEL + partner * share, share)
        swaps.append((acc.at[pl.ds(at, share)], got_prod.at[cycle]))
    swaps.append((acc.at[pl.ds(top, 2 * PANEL)], got_gram))
    copies = []
    for k, (source, target) in enumerate(swaps):
        copies.append(pltpu.make_async_remote_copy(
            src_ref=source, dst_ref=target, send_sem=swap_sem.at[0, k], recv_sem=swap_sem.at[1, k],
            device_id=(row, partner), device_id_type=MESH))
    for copy in copies:
        copy.start()
    for s in range(2):
        for t in range(TREES):
            for way in range(4):
                wanted = sends[s][t][way]
                if wanted is None:
                    continue

                @pl.when(wanted)
                def _():
                    whole = piece(s, t, 0, counts[t])
                    pltpu.make_async_remote_copy(
                        src_ref=whole, dst_ref=whole,
                        send_sem=send_sem.at[s, t, way], recv_sem=recv_sem.at[s, t, 0],
                        device_id=(targets[way], col), device_id_type=MESH,
                    ).wait_send()
    for copy in copies:
        copy.wait()
    for cycle in range(cycles):
        at = pl.multiple_of(cycle * PANEL + col * share, share)
        prod_ref[cycle] = acc[pl.ds(at, share)] + got_prod[cycle]
    gram_ref[...] = acc[top:] + got_gram[...]


def on_device(rows, factor, scales, coords, jitter):
    cycles, block_rows, width_local = factor.shape
    lead_width = 2 * PANEL
    col_count = lax.axis_size("col")
    share_rows = PANEL // col_count
    chunks = width_local // CHUNK
    pieces, gram_sum = pl.pallas_call(
        functools.partial(gather_products, rows),
        out_shape=(
            jax.ShapeDtypeStruct((cycles, share_rows, lead_width), jnp.float32),
            jax.ShapeDtypeStruct((lead_width, lead_width), jnp.float32),
        ),
        in_specs=[
            pl.BlockSpec(memory_space=pl.ANY),
            pl.BlockSpec(memory_space=pltpu.SMEM),
        ],
        out_specs=(
            pl.BlockSpec(memory_space=pltpu.VMEM),
            pl.BlockSpec(memory_space=pltpu.VMEM),
        ),
        scratch_shapes=[
            pltpu.VMEM((cycles, PANEL, width_local), jnp.bfloat16),
            pltpu.VMEM((2, chunks, PANEL, CHUNK), jnp.bfloat16),
            pltpu.VMEM((cycles * PANEL, PAIR * CHUNK), jnp.bfloat16),
            pltpu.VMEM((cycles * PANEL + lead_width, lead_width), jnp.float32),
            pltpu.VMEM((cycles, share_rows, lead_width), jnp.float32),
            pltpu.VMEM((lead_width, lead_width), jnp.float32),
            pltpu.SemaphoreType.DMA((TREES, 2)),
            pltpu.SemaphoreType.DMA((2, TREES, 4)),
            pltpu.SemaphoreType.DMA((2, TREES, max(counts_of(chunks)))),
            pltpu.SemaphoreType.DMA((2, cycles + 1)),
        ],
        compiler_params=pltpu.CompilerParams(
            collective_id=0, has_side_effects=True, vmem_limit_bytes=48 * 1024 * 1024),
        cost_estimate=pl.CostEstimate(
            flops=8 * cycles * PANEL * lead_width * width_local,
            bytes_accessed=factor.size * 2, transcendentals=0),
        name="gather_products",
    )(factor, scales.reshape(cycles, -1))
    row_index = lax.axis_index("row")
    col_index = lax.axis_index("col")
    row_count = lax.axis_size("row")
    own_pts = lax.dynamic_slice_in_dim(
        coords, row_index * PANEL + col_index * share_rows, share_rows, 2
    ).reshape(2, cycles * share_rows)
    lead_pts = coords[:, 0, :lead_width]
    local_rows = jnp.arange(cycles * share_rows, dtype=jnp.int32)
    global_rows = (
        local_rows // share_rows * (row_count * PANEL)
        + row_index * PANEL + col_index * share_rows + local_rows % share_rows
    )
    identity_mask = (
        global_rows[:, None] == jnp.arange(lead_width, dtype=jnp.int32)[None, :]
    ).astype(jnp.float32)
    kernel = matern(own_pts, lead_pts) + jitter[0] * identity_mask
    lead_kernel = matern(lead_pts, lead_pts) + jitter[0] * jnp.eye(lead_width, dtype=jnp.float32)
    solved = pl.pallas_call(
        solve_panels,
        out_shape=jax.ShapeDtypeStruct((cycles * share_rows, lead_width), jnp.float32),
        scratch_shapes=[pltpu.VMEM((PANEL, PANEL), jnp.float32)] * 3,
        compiler_params=pltpu.CompilerParams(vmem_limit_bytes=16 * 1024 * 1024),
        name="solve_panels",
    )(gram_sum, lead_kernel, pieces.reshape(cycles * share_rows, lead_width), kernel)
    return solved.reshape(cycles, share_rows, lead_width)


def solution(mesh):
    placed = (P(None, "row", "col"), P(None, "row", "col"), P(), P())
    return jax.shard_map(
        functools.partial(on_device, mesh.shape["row"]),
        mesh=mesh,
        in_specs=placed,
        out_specs=P(None, ("row", "col"), None),
        check_vma=False,
    )
```

```python
import functools
import jax
import jax.numpy as jnp
from jax import lax
from jax.experimental import pallas as pl
from jax.experimental.pallas import tpu as pltpu
from jax.sharding import PartitionSpec as P

PANEL = 128
CHUNK = 128
GROUP = 4
SKEW = 2
HEAD = 16

SQRT_THREE = 1.7320508075688772
LENGTH_SCALE = 0.25
MESH = pl.DeviceIdType.MESH
TREES = 3
TWIN, CHAIN, LIFT = 0, 2, 1


def matern(left_pts, right_pts):
    diff_x = left_pts[0][:, None] - right_pts[0][None, :]
    diff_y = left_pts[1][:, None] - right_pts[1][None, :]
    scaled = SQRT_THREE * jnp.sqrt(diff_x * diff_x + diff_y * diff_y) / LENGTH_SCALE
    return (1.0 + scaled) * jnp.exp(-scaled)


def exact_dot(left, right, transposed):
    dims = (((1,), (1 if transposed else 0,)), ((), ()))
    return lax.dot_general(
        left, right, dims, precision=lax.Precision.HIGHEST, preferred_element_type=jnp.float32
    )


def inverse_factor(block, out_ref):
    size = block.shape[0]
    tiles = size // 8
    sub = lax.broadcasted_iota(jnp.int32, (8, size), 0)
    lane = lax.broadcasted_iota(jnp.int32, (8, size), 1)
    left = [block[8 * k:8 * k + 8] for k in range(tiles)]
    right = [(lane == sub + 8 * k).astype(jnp.float32) for k in range(tiles)]
    for j in range(0, size, 2):
        home, r = j // 8, j % 8
        left_one, left_two = left[home][r:r + 1, :], left[home][r + 1:r + 2, :]
        right_one, right_two = right[home][r:r + 1, :], right[home][r + 1:r + 2, :]
        first = jnp.broadcast_to(left_one[:, j:j + 1], (1, size))
        cross = jnp.broadcast_to(left_one[:, j + 1:j + 2], (1, size))
        second = jnp.broadcast_to(left_two[:, j + 1:j + 2], (1, size))
        det = first * second - cross * cross
        lower = first * right_two - cross * right_one
        out_ref[j:j + 1, :] = right_one * lax.rsqrt(first)
        out_ref[j + 1:j + 2, :] = lower * lax.rsqrt(first * det)
        if j + 2 == size:
            break
        inverse = 1.0 / det
        solved_left = (
            (second * left_one - cross * left_two) * inverse,
            (first * left_two - cross * left_one) * inverse,
        )
        solved_right = (
            (second * right_one - cross * right_two) * inverse,
            lower * inverse,
        )
        for k in range(home, tiles):
            if k == home and r == 6:
                continue
            columns = [jnp.broadcast_to(left[k][:, j + m:j + m + 1], (8, size)) for m in range(2)]
            if k == home:
                columns = [jnp.where(sub > r + 1, column, 0.0) for column in columns]
            left[k] = left[k] - (columns[0] * solved_left[0] + columns[1] * solved_left[1])
            right[k] = right[k] - (columns[0] * solved_right[0] + columns[1] * solved_right[1])


def solve_panels(gram_ref, lead_ref, prod_ref, kernel_ref, out_ref, block, inv_one, inv_two):
    half = block.shape[0]
    block[...] = lead_ref[:half, :half] - gram_ref[:half, :half]
    inverse_factor(block[...], inv_one)
    first = inv_one[...]
    below = exact_dot(lead_ref[half:, :half] - gram_ref[half:, :half], first, True)
    block[...] = lead_ref[half:, half:] - gram_ref[half:, half:] - exact_dot(below, below, True)
    one = exact_dot(kernel_ref[:, :half] - prod_ref[:, :half], first, True)
    rest = kernel_ref[:, half:] - prod_ref[:, half:] - exact_dot(one, below, True)
    inverse_factor(block[...], inv_two)
    out_ref[:, :half] = one
    out_ref[:, half:] = exact_dot(rest, inv_two[...], True)


def counts_of(chunks):
    groups = chunks // GROUP
    return [GROUP * (groups // TREES + (1 if t < groups % TREES else 0)) for t in range(TREES)]


def roles(tree, xs, y, z, planes):
    top = z == planes - 1
    low = z == 0
    a = (xs == 0) & (y == 0)
    b = (xs == 1) & (y == 0)
    c = (xs == 1) & (y == 1)
    d = (xs == 0) & (y == 1)
    up = jnp.logical_not(top)
    if tree == TWIN:
        return z + y + xs, xs == 0, a & low, (xs == 0) & up, None
    high = jnp.logical_not(low)
    if tree == CHAIN:
        place = jnp.where(d, 1, jnp.where(a, 2, jnp.where(b, 3, 4)))
        depth = jnp.where(low, xs + y, z + place)
        send_x = (low & (xs == 0)) | (high & a)
        send_y = (low & a) | (high & (d | b))
        return depth, send_x, send_y, d & up, None
    place = jnp.where(a, 0, jnp.where(d, 1, jnp.where(c, 2, 3)))
    depth = jnp.where(low, jnp.where(a, 0, place + 2), z + place)
    return depth, high & d, high & (a | c), a & up, (z == 1) & jnp.logical_not(a)


def gather_products(rows, factor_hbm, scales_ref, prod_ref, gram_ref,
                    raw, lead, lhs, acc, got_prod, got_gram,
                    load_sem, send_sem, recv_sem, swap_sem):
    cycles, _, width = raw.shape
    row = lax.axis_index("row")
    col = lax.axis_index("col")
    chunks = width // CHUNK
    counts = counts_of(chunks)
    starts = [sum(counts[:t]) for t in range(TREES)]
    planes = rows // 4
    x = row % 2
    y = (row // 2) % 2
    z = row // 4
    targets = [
        row + 1 - 2 * x,
        row + 2 - 4 * y,
        jnp.minimum(row + 4, rows - 1),
        jnp.maximum(row - 4, 0),
    ]
    has_up = z < planes - 1
    has_down = z > 0
    partner = 1 - col

    head = min(HEAD, min(counts) - GROUP)
    loads = []
    for t in range(TREES):
        for part, (low, size) in enumerate(((0, head), (head, counts[t] - head))):
            span = pl.ds((starts[t] + low) * CHUNK, size * CHUNK)
            loads.append(pltpu.make_async_copy(
                factor_hbm.at[:, :, span], raw.at[:, :, span], load_sem.at[t, part]))
    for t in range(TREES):
        loads[2 * t].start()
    for t in range(TREES):
        loads[2 * t + 1].start()

    barrier = pltpu.get_barrier_semaphore()

    def greet(target):
        pl.semaphore_signal(barrier, inc=1, device_id=target, device_id_type=MESH)

    greet((targets[0], col))
    greet((targets[1], col))
    greet((row, partner))
    pl.when(has_up)(lambda: greet((targets[2], col)))
    pl.when(has_down)(lambda: greet((targets[3], col)))
    acc[...] = jnp.zeros_like(acc)
    pl.semaphore_wait(barrier, 3 + has_up.astype(jnp.int32) + has_down.astype(jnp.int32))

    depths = [[None] * TREES for _ in range(2)]
    sends = [[None] * TREES for _ in range(2)]
    for s in range(2):
        xs = x if s == 0 else 1 - x
        for t in range(TREES):
            depth, *send = roles(t, xs, y, z, planes)
            depths[s][t] = depth
            sends[s][t] = send
    deepest = [planes + 1, planes + 2, planes + 3]
    delays = [2, 1, 0]
    steps = max(counts[t] + SKEW * deepest[t] + delays[t] for t in range(TREES))

    def piece(s, t, index, size=1):
        return lead.at[s, pl.ds(starts[t] + index, size)]

    def dequantize(cycle, chunk):
        at = pl.multiple_of(chunk * CHUNK, CHUNK)
        block = raw[cycle, :, pl.ds(at, CHUNK)].astype(jnp.float32) * scales_ref[cycle, chunk]
        return block.astype(jnp.bfloat16)

    def forward(s, t, step):
        index = step - SKEW * depths[s][t]

        @pl.when((index >= 0) & (index < counts[t]))
        def _():
            here = piece(s, t, index)

            @pl.when(row == s)
            def _():
                lead[s, starts[t] + index] = dequantize(0, starts[t] + index)

            @pl.when(row != s)
            def _():
                pltpu.make_async_copy(here, here, recv_sem.at[s, t, index]).wait()

            for way in range(4):
                wanted = sends[s][t][way]
                if wanted is None:
                    continue

                @pl.when(wanted)
                def _():
                    pltpu.make_async_remote_copy(
                        src_ref=here, dst_ref=here,
                        send_sem=send_sem.at[s, t, way], recv_sem=recv_sem.at[s, t, index],
                        device_id=(targets[way], col), device_id_type=MESH,
                    ).start()

    def multiply(t, step):
        index = step - SKEW * jnp.maximum(depths[0][t], depths[1][t]) - delays[t]

        @pl.when((index >= 0) & (index < counts[t]) & (index % GROUP == GROUP - 1))
        def _():
            first = starts[t] + index - (GROUP - 1)
            for cycle in range(cycles):
                for b in range(GROUP):
                    lhs[cycle * PANEL:(cycle + 1) * PANEL, b * CHUNK:(b + 1) * CHUNK] = (
                        dequantize(cycle, first + b))
            right = jnp.concatenate([
                jnp.concatenate([lead[s, first + b] for b in range(GROUP)], axis=1)
                for s in range(2)], axis=0)
            dims = (((1,), (1,)), ((), ()))
            own = jnp.concatenate([lhs[...], right], axis=0)
            acc[...] += lax.dot_general(own, right, dims, preferred_element_type=jnp.float32)

    def one_step(step, carry):
        for t in range(TREES):
            for s in range(2):
                forward(s, t, step)
        for t in range(TREES):
            multiply(t, step)
        return carry

    for t in range(TREES):
        loads[2 * t].wait()
    lax.fori_loop(0, head, one_step, 0)
    for t in range(TREES):
        loads[2 * t + 1].wait()
    lax.fori_loop(head, steps, one_step, 0)

    share = PANEL // 2
    top = cycles * PANEL
    swaps = []
    for cycle in range(cycles):
        at = pl.multiple_of(cycle * PANEL + partner * share, share)
        swaps.append((acc.at[pl.ds(at, share)], got_prod.at[cycle]))
    swaps.append((acc.at[pl.ds(top, 2 * PANEL)], got_gram))
    copies = []
    for k, (source, target) in enumerate(swaps):
        copies.append(pltpu.make_async_remote_copy(
            src_ref=source, dst_ref=target, send_sem=swap_sem.at[0, k], recv_sem=swap_sem.at[1, k],
            device_id=(row, partner), device_id_type=MESH))
    for copy in copies:
        copy.start()
    for s in range(2):
        for t in range(TREES):
            for way in range(4):
                wanted = sends[s][t][way]
                if wanted is None:
                    continue

                @pl.when(wanted)
                def _():
                    whole = piece(s, t, 0, counts[t])
                    pltpu.make_async_remote_copy(
                        src_ref=whole, dst_ref=whole,
                        send_sem=send_sem.at[s, t, way], recv_sem=recv_sem.at[s, t, 0],
                        device_id=(targets[way], col), device_id_type=MESH,
                    ).wait_send()
    for copy in copies:
        copy.wait()
    for cycle in range(cycles):
        at = pl.multiple_of(cycle * PANEL + col * share, share)
        prod_ref[cycle] = acc[pl.ds(at, share)] + got_prod[cycle]
    gram_ref[...] = acc[top:] + got_gram[...]


def on_device(rows, factor, scales, coords, jitter):
    cycles, block_rows, width_local = factor.shape
    lead_width = 2 * PANEL
    col_count = lax.axis_size("col")
    share_rows = PANEL // col_count
    chunks = width_local // CHUNK
    pieces, gram_sum = pl.pallas_call(
        functools.partial(gather_products, rows),
        out_shape=(
            jax.ShapeDtypeStruct((cycles, share_rows, lead_width), jnp.float32),
            jax.ShapeDtypeStruct((lead_width, lead_width), jnp.float32),
        ),
        in_specs=[
            pl.BlockSpec(memory_space=pl.ANY),
            pl.BlockSpec(memory_space=pltpu.SMEM),
        ],
        out_specs=(
            pl.BlockSpec(memory_space=pltpu.VMEM),
            pl.BlockSpec(memory_space=pltpu.VMEM),
        ),
        scratch_shapes=[
            pltpu.VMEM((cycles, PANEL, width_local), jnp.bfloat16),
            pltpu.VMEM((2, chunks, PANEL, CHUNK), jnp.bfloat16),
            pltpu.VMEM((cycles * PANEL, GROUP * CHUNK), jnp.bfloat16),
            pltpu.VMEM((cycles * PANEL + lead_width, lead_width), jnp.float32),
            pltpu.VMEM((cycles, share_rows, lead_width), jnp.float32),
            pltpu.VMEM((lead_width, lead_width), jnp.float32),
            pltpu.SemaphoreType.DMA((TREES, 2)),
            pltpu.SemaphoreType.DMA((2, TREES, 4)),
            pltpu.SemaphoreType.DMA((2, TREES, max(counts_of(chunks)))),
            pltpu.SemaphoreType.DMA((2, cycles + 1)),
        ],
        compiler_params=pltpu.CompilerParams(
            collective_id=0, has_side_effects=True, vmem_limit_bytes=48 * 1024 * 1024),
        cost_estimate=pl.CostEstimate(
            flops=8 * cycles * PANEL * lead_width * width_local,
            bytes_accessed=factor.size * 2, transcendentals=0),
        name="gather_products",
    )(factor, scales.reshape(cycles, -1))
    row_index = lax.axis_index("row")
    col_index = lax.axis_index("col")
    row_count = lax.axis_size("row")
    own_pts = lax.dynamic_slice_in_dim(
        coords, row_index * PANEL + col_index * share_rows, share_rows, 2
    ).reshape(2, cycles * share_rows)
    lead_pts = coords[:, 0, :lead_width]
    local_rows = jnp.arange(cycles * share_rows, dtype=jnp.int32)
    global_rows = (
        local_rows // share_rows * (row_count * PANEL)
        + row_index * PANEL + col_index * share_rows + local_rows % share_rows
    )
    identity_mask = (
        global_rows[:, None] == jnp.arange(lead_width, dtype=jnp.int32)[None, :]
    ).astype(jnp.float32)
    kernel = matern(own_pts, lead_pts) + jitter[0] * identity_mask
    lead_kernel = matern(lead_pts, lead_pts) + jitter[0] * jnp.eye(lead_width, dtype=jnp.float32)
    solved = pl.pallas_call(
        solve_panels,
        out_shape=jax.ShapeDtypeStruct((cycles * share_rows, lead_width), jnp.float32),
        scratch_shapes=[pltpu.VMEM((PANEL, PANEL), jnp.float32)] * 3,
        compiler_params=pltpu.CompilerParams(vmem_limit_bytes=16 * 1024 * 1024),
        name="solve_panels",
    )(gram_sum, lead_kernel, pieces.reshape(cycles * share_rows, lead_width), kernel)
    return solved.reshape(cycles, share_rows, lead_width)


def solution(mesh):
    placed = (P(None, "row", "col"), P(None, "row", "col"), P(), P())
    return jax.shard_map(
        functools.partial(on_device, mesh.shape["row"]),
        mesh=mesh,
        in_specs=placed,
        out_specs=P(None, ("row", "col"), None),
        check_vma=False,
    )
```

```python
import functools
import jax
import jax.numpy as jnp
from jax import lax
from jax.experimental import pallas as pl
from jax.experimental.pallas import tpu as pltpu
from jax.sharding import PartitionSpec as P

PANEL = 128
CHUNK = 128
GROUP = 4
SKEW = 3
HEAD = 16

SQRT_THREE = 1.7320508075688772
LENGTH_SCALE = 0.25
MESH = pl.DeviceIdType.MESH
TREES = 3
TWIN, CHAIN, LIFT = 0, 2, 1


def matern(left_pts, right_pts):
    diff_x = left_pts[0][:, None] - right_pts[0][None, :]
    diff_y = left_pts[1][:, None] - right_pts[1][None, :]
    scaled = SQRT_THREE * jnp.sqrt(diff_x * diff_x + diff_y * diff_y) / LENGTH_SCALE
    return (1.0 + scaled) * jnp.exp(-scaled)


def exact_dot(left, right, transposed):
    dims = (((1,), (1 if transposed else 0,)), ((), ()))
    return lax.dot_general(
        left, right, dims, precision=lax.Precision.HIGHEST, preferred_element_type=jnp.float32
    )


def inverse_factor(block, out_ref):
    size = block.shape[0]
    tiles = size // 8
    sub = lax.broadcasted_iota(jnp.int32, (8, size), 0)
    lane = lax.broadcasted_iota(jnp.int32, (8, size), 1)
    left = [block[8 * k:8 * k + 8] for k in range(tiles)]
    right = [(lane == sub + 8 * k).astype(jnp.float32) for k in range(tiles)]
    for j in range(0, size, 2):
        home, r = j // 8, j % 8
        left_one, left_two = left[home][r:r + 1, :], left[home][r + 1:r + 2, :]
        right_one, right_two = right[home][r:r + 1, :], right[home][r + 1:r + 2, :]
        first = jnp.broadcast_to(left_one[:, j:j + 1], (1, size))
        cross = jnp.broadcast_to(left_one[:, j + 1:j + 2], (1, size))
        second = jnp.broadcast_to(left_two[:, j + 1:j + 2], (1, size))
        det = first * second - cross * cross
        lower = first * right_two - cross * right_one
        out_ref[j:j + 1, :] = right_one * lax.rsqrt(first)
        out_ref[j + 1:j + 2, :] = lower * lax.rsqrt(first * det)
        if j + 2 == size:
            break
        inverse = 1.0 / det
        solved_left = (
            (second * left_one - cross * left_two) * inverse,
            (first * left_two - cross * left_one) * inverse,
        )
        solved_right = (
            (second * right_one - cross * right_two) * inverse,
            lower * inverse,
        )
        for k in range(home, tiles):
            if k == home and r == 6:
                continue
            columns = [jnp.broadcast_to(left[k][:, j + m:j + m + 1], (8, size)) for m in range(2)]
            if k == home:
                columns = [jnp.where(sub > r + 1, column, 0.0) for column in columns]
            left[k] = left[k] - (columns[0] * solved_left[0] + columns[1] * solved_left[1])
            right[k] = right[k] - (columns[0] * solved_right[0] + columns[1] * solved_right[1])


def solve_panels(gram_ref, lead_ref, prod_ref, kernel_ref, out_ref, block, inv_one, inv_two):
    half = block.shape[0]
    block[...] = lead_ref[:half, :half] - gram_ref[:half, :half]
    inverse_factor(block[...], inv_one)
    first = inv_one[...]
    below = exact_dot(lead_ref[half:, :half] - gram_ref[half:, :half], first, True)
    block[...] = lead_ref[half:, half:] - gram_ref[half:, half:] - exact_dot(below, below, True)
    one = exact_dot(kernel_ref[:, :half] - prod_ref[:, :half], first, True)
    rest = kernel_ref[:, half:] - prod_ref[:, half:] - exact_dot(one, below, True)
    inverse_factor(block[...], inv_two)
    out_ref[:, :half] = one
    out_ref[:, half:] = exact_dot(rest, inv_two[...], True)


def counts_of(chunks):
    groups = chunks // GROUP
    return [GROUP * (groups // TREES + (1 if t < groups % TREES else 0)) for t in range(TREES)]


def roles(tree, xs, y, z, planes):
    top = z == planes - 1
    low = z == 0
    a = (xs == 0) & (y == 0)
    b = (xs == 1) & (y == 0)
    c = (xs == 1) & (y == 1)
    d = (xs == 0) & (y == 1)
    up = jnp.logical_not(top)
    if tree == TWIN:
        return z + y + xs, xs == 0, a & low, (xs == 0) & up, None
    high = jnp.logical_not(low)
    if tree == CHAIN:
        place = jnp.where(d, 1, jnp.where(a, 2, jnp.where(b, 3, 4)))
        depth = jnp.where(low, xs + y, z + place)
        send_x = (low & (xs == 0)) | (high & a)
        send_y = (low & a) | (high & (d | b))
        return depth, send_x, send_y, d & up, None
    place = jnp.where(a, 0, jnp.where(d, 1, jnp.where(c, 2, 3)))
    depth = jnp.where(low, jnp.where(a, 0, place + 2), z + place)
    return depth, high & d, high & (a | c), a & up, (z == 1) & jnp.logical_not(a)


def gather_products(rows, factor_hbm, scales_ref, prod_ref, gram_ref,
                    raw, lead, lhs, acc, got_prod, got_gram,
                    load_sem, send_sem, recv_sem, swap_sem):
    cycles, _, width = raw.shape
    row = lax.axis_index("row")
    col = lax.axis_index("col")
    chunks = width // CHUNK
    counts = counts_of(chunks)
    starts = [sum(counts[:t]) for t in range(TREES)]
    planes = rows // 4
    x = row % 2
    y = (row // 2) % 2
    z = row // 4
    targets = [
        row + 1 - 2 * x,
        row + 2 - 4 * y,
        jnp.minimum(row + 4, rows - 1),
        jnp.maximum(row - 4, 0),
    ]
    has_up = z < planes - 1
    has_down = z > 0
    partner = 1 - col

    head = min(HEAD, min(counts) - GROUP)
    loads = []
    for t in range(TREES):
        for part, (low, size) in enumerate(((0, head), (head, counts[t] - head))):
            span = pl.ds((starts[t] + low) * CHUNK, size * CHUNK)
            loads.append(pltpu.make_async_copy(
                factor_hbm.at[:, :, span], raw.at[:, :, span], load_sem.at[t, part]))
    for t in range(TREES):
        loads[2 * t].start()
    for t in range(TREES):
        loads[2 * t + 1].start()

    barrier = pltpu.get_barrier_semaphore()

    def greet(target):
        pl.semaphore_signal(barrier, inc=1, device_id=target, device_id_type=MESH)

    greet((targets[0], col))
    greet((targets[1], col))
    greet((row, partner))
    pl.when(has_up)(lambda: greet((targets[2], col)))
    pl.when(has_down)(lambda: greet((targets[3], col)))
    acc[...] = jnp.zeros_like(acc)
    pl.semaphore_wait(barrier, 3 + has_up.astype(jnp.int32) + has_down.astype(jnp.int32))

    depths = [[None] * TREES for _ in range(2)]
    sends = [[None] * TREES for _ in range(2)]
    for s in range(2):
        xs = x if s == 0 else 1 - x
        for t in range(TREES):
            depth, *send = roles(t, xs, y, z, planes)
            depths[s][t] = depth
            sends[s][t] = send
    deepest = [planes + 1, planes + 2, planes + 3]
    delays = [2, 1, 0]
    steps = max(counts[t] + SKEW * deepest[t] + delays[t] for t in range(TREES))

    def piece(s, t, index, size=1):
        return lead.at[s, pl.ds(starts[t] + index, size)]

    def dequantize(cycle, chunk):
        at = pl.multiple_of(chunk * CHUNK, CHUNK)
        block = raw[cycle, :, pl.ds(at, CHUNK)].astype(jnp.float32) * scales_ref[cycle, chunk]
        return block.astype(jnp.bfloat16)

    def forward(s, t, step):
        index = step - SKEW * depths[s][t]

        @pl.when((index >= 0) & (index < counts[t]))
        def _():
            here = piece(s, t, index)

            @pl.when(row == s)
            def _():
                lead[s, starts[t] + index] = dequantize(0, starts[t] + index)

            @pl.when(row != s)
            def _():
                pltpu.make_async_copy(here, here, recv_sem.at[s, t, index]).wait()

            for way in range(4):
                wanted = sends[s][t][way]
                if wanted is None:
                    continue

                @pl.when(wanted)
                def _():
                    pltpu.make_async_remote_copy(
                        src_ref=here, dst_ref=here,
                        send_sem=send_sem.at[s, t, way], recv_sem=recv_sem.at[s, t, index],
                        device_id=(targets[way], col), device_id_type=MESH,
                    ).start()

    def multiply(t, step):
        index = step - SKEW * jnp.maximum(depths[0][t], depths[1][t]) - delays[t]

        @pl.when((index >= 0) & (index < counts[t]) & (index % GROUP == GROUP - 1))
        def _():
            first = starts[t] + index - (GROUP - 1)
            for cycle in range(cycles):
                for b in range(GROUP):
                    lhs[cycle * PANEL:(cycle + 1) * PANEL, b * CHUNK:(b + 1) * CHUNK] = (
                        dequantize(cycle, first + b))
            right = jnp.concatenate([
                jnp.concatenate([lead[s, first + b] for b in range(GROUP)], axis=1)
                for s in range(2)], axis=0)
            dims = (((1,), (1,)), ((), ()))
            own = jnp.concatenate([lhs[...], right], axis=0)
            acc[...] += lax.dot_general(own, right, dims, preferred_element_type=jnp.float32)

    def one_step(step, carry):
        for t in range(TREES):
            for s in range(2):
                forward(s, t, step)
        for t in range(TREES):
            multiply(t, step)
        return carry

    for t in range(TREES):
        loads[2 * t].wait()
    lax.fori_loop(0, head, one_step, 0)
    for t in range(TREES):
        loads[2 * t + 1].wait()
    lax.fori_loop(head, steps, one_step, 0)

    share = PANEL // 2
    top = cycles * PANEL
    swaps = []
    for cycle in range(cycles):
        at = pl.multiple_of(cycle * PANEL + partner * share, share)
        swaps.append((acc.at[pl.ds(at, share)], got_prod.at[cycle]))
    swaps.append((acc.at[pl.ds(top, 2 * PANEL)], got_gram))
    copies = []
    for k, (source, target) in enumerate(swaps):
        copies.append(pltpu.make_async_remote_copy(
            src_ref=source, dst_ref=target, send_sem=swap_sem.at[0, k], recv_sem=swap_sem.at[1, k],
            device_id=(row, partner), device_id_type=MESH))
    for copy in copies:
        copy.start()
    for s in range(2):
        for t in range(TREES):
            for way in range(4):
                wanted = sends[s][t][way]
                if wanted is None:
                    continue

                @pl.when(wanted)
                def _():
                    whole = piece(s, t, 0, counts[t])
                    pltpu.make_async_remote_copy(
                        src_ref=whole, dst_ref=whole,
                        send_sem=send_sem.at[s, t, way], recv_sem=recv_sem.at[s, t, 0],
                        device_id=(targets[way], col), device_id_type=MESH,
                    ).wait_send()
    for copy in copies:
        copy.wait()
    for cycle in range(cycles):
        at = pl.multiple_of(cycle * PANEL + col * share, share)
        prod_ref[cycle] = acc[pl.ds(at, share)] + got_prod[cycle]
    gram_ref[...] = acc[top:] + got_gram[...]


def on_device(rows, factor, scales, coords, jitter):
    cycles, block_rows, width_local = factor.shape
    lead_width = 2 * PANEL
    col_count = lax.axis_size("col")
    share_rows = PANEL // col_count
    chunks = width_local // CHUNK
    pieces, gram_sum = pl.pallas_call(
        functools.partial(gather_products, rows),
        out_shape=(
            jax.ShapeDtypeStruct((cycles, share_rows, lead_width), jnp.float32),
            jax.ShapeDtypeStruct((lead_width, lead_width), jnp.float32),
        ),
        in_specs=[
            pl.BlockSpec(memory_space=pl.ANY),
            pl.BlockSpec(memory_space=pltpu.SMEM),
        ],
        out_specs=(
            pl.BlockSpec(memory_space=pltpu.VMEM),
            pl.BlockSpec(memory_space=pltpu.VMEM),
        ),
        scratch_shapes=[
            pltpu.VMEM((cycles, PANEL, width_local), jnp.bfloat16),
            pltpu.VMEM((2, chunks, PANEL, CHUNK), jnp.bfloat16),
            pltpu.VMEM((cycles * PANEL, GROUP * CHUNK), jnp.bfloat16),
            pltpu.VMEM((cycles * PANEL + lead_width, lead_width), jnp.float32),
            pltpu.VMEM((cycles, share_rows, lead_width), jnp.float32),
            pltpu.VMEM((lead_width, lead_width), jnp.float32),
            pltpu.SemaphoreType.DMA((TREES, 2)),
            pltpu.SemaphoreType.DMA((2, TREES, 4)),
            pltpu.SemaphoreType.DMA((2, TREES, max(counts_of(chunks)))),
            pltpu.SemaphoreType.DMA((2, cycles + 1)),
        ],
        compiler_params=pltpu.CompilerParams(
            collective_id=0, has_side_effects=True, vmem_limit_bytes=48 * 1024 * 1024),
        cost_estimate=pl.CostEstimate(
            flops=8 * cycles * PANEL * lead_width * width_local,
            bytes_accessed=factor.size * 2, transcendentals=0),
        name="gather_products",
    )(factor, scales.reshape(cycles, -1))
    row_index = lax.axis_index("row")
    col_index = lax.axis_index("col")
    row_count = lax.axis_size("row")
    own_pts = lax.dynamic_slice_in_dim(
        coords, row_index * PANEL + col_index * share_rows, share_rows, 2
    ).reshape(2, cycles * share_rows)
    lead_pts = coords[:, 0, :lead_width]
    local_rows = jnp.arange(cycles * share_rows, dtype=jnp.int32)
    global_rows = (
        local_rows // share_rows * (row_count * PANEL)
        + row_index * PANEL + col_index * share_rows + local_rows % share_rows
    )
    identity_mask = (
        global_rows[:, None] == jnp.arange(lead_width, dtype=jnp.int32)[None, :]
    ).astype(jnp.float32)
    kernel = matern(own_pts, lead_pts) + jitter[0] * identity_mask
    lead_kernel = matern(lead_pts, lead_pts) + jitter[0] * jnp.eye(lead_width, dtype=jnp.float32)
    solved = pl.pallas_call(
        solve_panels,
        out_shape=jax.ShapeDtypeStruct((cycles * share_rows, lead_width), jnp.float32),
        scratch_shapes=[pltpu.VMEM((PANEL, PANEL), jnp.float32)] * 3,
        compiler_params=pltpu.CompilerParams(vmem_limit_bytes=16 * 1024 * 1024),
        name="solve_panels",
    )(gram_sum, lead_kernel, pieces.reshape(cycles * share_rows, lead_width), kernel)
    return solved.reshape(cycles, share_rows, lead_width)


def solution(mesh):
    placed = (P(None, "row", "col"), P(None, "row", "col"), P(), P())
    return jax.shard_map(
        functools.partial(on_device, mesh.shape["row"]),
        mesh=mesh,
        in_specs=placed,
        out_specs=P(None, ("row", "col"), None),
        check_vma=False,
    )
```

```python
import functools
import jax
import jax.numpy as jnp
from jax import lax
from jax.experimental import pallas as pl
from jax.experimental.pallas import tpu as pltpu
from jax.sharding import PartitionSpec as P

PANEL = 128
CHUNK = 128
GROUP = 4
SKEW = 3
HEAD = 16

SQRT_THREE = 1.7320508075688772
LENGTH_SCALE = 0.25
MESH = pl.DeviceIdType.MESH
TREES = 3
TWIN, CHAIN, LIFT = 0, 2, 1


def matern(left_pts, right_pts):
    diff_x = left_pts[0][:, None] - right_pts[0][None, :]
    diff_y = left_pts[1][:, None] - right_pts[1][None, :]
    scaled = SQRT_THREE * jnp.sqrt(diff_x * diff_x + diff_y * diff_y) / LENGTH_SCALE
    return (1.0 + scaled) * jnp.exp(-scaled)


def exact_dot(left, right, transposed):
    dims = (((1,), (1 if transposed else 0,)), ((), ()))
    return lax.dot_general(
        left, right, dims, precision=lax.Precision.HIGHEST, preferred_element_type=jnp.float32
    )


def inverse_factor(block, out_ref):
    size = block.shape[0]
    tiles = size // 8
    sub = lax.broadcasted_iota(jnp.int32, (8, size), 0)
    lane = lax.broadcasted_iota(jnp.int32, (8, size), 1)
    left = [block[8 * k:8 * k + 8] for k in range(tiles)]
    right = [(lane == sub + 8 * k).astype(jnp.float32) for k in range(tiles)]
    for j in range(0, size, 2):
        home, r = j // 8, j % 8
        left_one, left_two = left[home][r:r + 1, :], left[home][r + 1:r + 2, :]
        right_one, right_two = right[home][r:r + 1, :], right[home][r + 1:r + 2, :]
        first = jnp.broadcast_to(left_one[:, j:j + 1], (1, size))
        cross = jnp.broadcast_to(left_one[:, j + 1:j + 2], (1, size))
        second = jnp.broadcast_to(left_two[:, j + 1:j + 2], (1, size))
        det = first * second - cross * cross
        lower = first * right_two - cross * right_one
        out_ref[j:j + 1, :] = right_one * lax.rsqrt(first)
        out_ref[j + 1:j + 2, :] = lower * lax.rsqrt(first * det)
        if j + 2 == size:
            break
        inverse = 1.0 / det
        solved_left = (
            (second * left_one - cross * left_two) * inverse,
            (first * left_two - cross * left_one) * inverse,
        )
        solved_right = (
            (second * right_one - cross * right_two) * inverse,
            lower * inverse,
        )
        for k in range(home, tiles):
            if k == home and r == 6:
                continue
            columns = [jnp.broadcast_to(left[k][:, j + m:j + m + 1], (8, size)) for m in range(2)]
            if k == home:
                columns = [jnp.where(sub > r + 1, column, 0.0) for column in columns]
            left[k] = left[k] - (columns[0] * solved_left[0] + columns[1] * solved_left[1])
            right[k] = right[k] - (columns[0] * solved_right[0] + columns[1] * solved_right[1])


def solve_panels(gram_ref, lead_ref, prod_ref, kernel_ref, out_ref, block, inv_one, inv_two):
    half = block.shape[0]
    block[...] = lead_ref[:half, :half] - gram_ref[:half, :half]
    inverse_factor(block[...], inv_one)
    first = inv_one[...]
    below = exact_dot(lead_ref[half:, :half] - gram_ref[half:, :half], first, True)
    block[...] = lead_ref[half:, half:] - gram_ref[half:, half:] - exact_dot(below, below, True)
    one = exact_dot(kernel_ref[:, :half] - prod_ref[:, :half], first, True)
    rest = kernel_ref[:, half:] - prod_ref[:, half:] - exact_dot(one, below, True)
    inverse_factor(block[...], inv_two)
    out_ref[:, :half] = one
    out_ref[:, half:] = exact_dot(rest, inv_two[...], True)


def counts_of(chunks):
    groups = chunks // GROUP
    return [GROUP * (groups // TREES + (1 if t < groups % TREES else 0)) for t in range(TREES)]


def roles(tree, xs, y, z, planes):
    top = z == planes - 1
    low = z == 0
    a = (xs == 0) & (y == 0)
    b = (xs == 1) & (y == 0)
    c = (xs == 1) & (y == 1)
    d = (xs == 0) & (y == 1)
    up = jnp.logical_not(top)
    if tree == TWIN:
        return z + y + xs, xs == 0, a & low, (xs == 0) & up, None
    high = jnp.logical_not(low)
    if tree == CHAIN:
        depth = jnp.where(low, xs + y, z + jnp.where(d, 1, jnp.where(b, 3, 2)))
        send_x = (low & (xs == 0)) | (high & d)
        send_y = (low & a) | (high & (d | c))
        return depth, send_x, send_y, d & up, None
    place = jnp.where(a, 0, jnp.where(c, 2, 1))
    depth = jnp.where(low, jnp.where(a, 0, place + 2), z + place)
    return depth, high & a, high & (a | b), a & up, (z == 1) & jnp.logical_not(a)


def gather_products(rows, factor_hbm, scales_ref, prod_ref, gram_ref,
                    raw, lead, lhs, acc, got_prod, got_gram,
                    load_sem, send_sem, recv_sem, swap_sem):
    cycles, _, width = raw.shape
    row = lax.axis_index("row")
    col = lax.axis_index("col")
    chunks = width // CHUNK
    counts = counts_of(chunks)
    starts = [sum(counts[:t]) for t in range(TREES)]
    planes = rows // 4
    x = row % 2
    y = (row // 2) % 2
    z = row // 4
    targets = [
        row + 1 - 2 * x,
        row + 2 - 4 * y,
        jnp.minimum(row + 4, rows - 1),
        jnp.maximum(row - 4, 0),
    ]
    has_up = z < planes - 1
    has_down = z > 0
    partner = 1 - col

    head = min(HEAD, min(counts) - GROUP)
    loads = []
    for t in range(TREES):
        for part, (low, size) in enumerate(((0, head), (head, counts[t] - head))):
            span = pl.ds((starts[t] + low) * CHUNK, size * CHUNK)
            loads.append(pltpu.make_async_copy(
                factor_hbm.at[:, :, span], raw.at[:, :, span], load_sem.at[t, part]))
    for t in range(TREES):
        loads[2 * t].start()
    for t in range(TREES):
        loads[2 * t + 1].start()

    barrier = pltpu.get_barrier_semaphore()

    def greet(target):
        pl.semaphore_signal(barrier, inc=1, device_id=target, device_id_type=MESH)

    greet((targets[0], col))
    greet((targets[1], col))
    greet((row, partner))
    pl.when(has_up)(lambda: greet((targets[2], col)))
    pl.when(has_down)(lambda: greet((targets[3], col)))
    acc[...] = jnp.zeros_like(acc)
    pl.semaphore_wait(barrier, 3 + has_up.astype(jnp.int32) + has_down.astype(jnp.int32))

    depths = [[None] * TREES for _ in range(2)]
    sends = [[None] * TREES for _ in range(2)]
    for s in range(2):
        xs = x if s == 0 else 1 - x
        for t in range(TREES):
            depth, *send = roles(t, xs, y, z, planes)
            depths[s][t] = depth
            sends[s][t] = send
    deepest = [planes + 1, planes + 1, planes + 2]
    delays = [0, 1, 0]
    steps = max(counts[t] + SKEW * deepest[t] + delays[t] for t in range(TREES))

    def piece(s, t, index, size=1):
        return lead.at[s, pl.ds(starts[t] + index, size)]

    def dequantize(cycle, chunk):
        at = pl.multiple_of(chunk * CHUNK, CHUNK)
        block = raw[cycle, :, pl.ds(at, CHUNK)].astype(jnp.float32) * scales_ref[cycle, chunk]
        return block.astype(jnp.bfloat16)

    def forward(s, t, step):
        index = step - SKEW * depths[s][t]

        @pl.when((index >= 0) & (index < counts[t]))
        def _():
            here = piece(s, t, index)

            @pl.when(row == s)
            def _():
                lead[s, starts[t] + index] = dequantize(0, starts[t] + index)

            @pl.when(row != s)
            def _():
                pltpu.make_async_copy(here, here, recv_sem.at[s, t, index]).wait()

            for way in range(4):
                wanted = sends[s][t][way]
                if wanted is None:
                    continue

                @pl.when(wanted)
                def _():
                    pltpu.make_async_remote_copy(
                        src_ref=here, dst_ref=here,
                        send_sem=send_sem.at[s, t, way], recv_sem=recv_sem.at[s, t, index],
                        device_id=(targets[way], col), device_id_type=MESH,
                    ).start()

    def multiply(t, step):
        index = step - SKEW * jnp.maximum(depths[0][t], depths[1][t]) - delays[t]

        @pl.when((index >= 0) & (index < counts[t]) & (index % GROUP == GROUP - 1))
        def _():
            first = starts[t] + index - (GROUP - 1)
            for cycle in range(cycles):
                for b in range(GROUP):
                    lhs[cycle * PANEL:(cycle + 1) * PANEL, b * CHUNK:(b + 1) * CHUNK] = (
                        dequantize(cycle, first + b))
            right = jnp.concatenate([
                jnp.concatenate([lead[s, first + b] for b in range(GROUP)], axis=1)
                for s in range(2)], axis=0)
            dims = (((1,), (1,)), ((), ()))
            own = jnp.concatenate([lhs[...], right], axis=0)
            acc[...] += lax.dot_general(own, right, dims, preferred_element_type=jnp.float32)

    def one_step(step, carry):
        for t in range(TREES):
            for s in range(2):
                forward(s, t, step)
        for t in range(TREES):
            multiply(t, step)
        return carry

    for t in range(TREES):
        loads[2 * t].wait()
    lax.fori_loop(0, head, one_step, 0)
    for t in range(TREES):
        loads[2 * t + 1].wait()
    lax.fori_loop(head, steps, one_step, 0)

    share = PANEL // 2
    top = cycles * PANEL
    swaps = []
    for cycle in range(cycles):
        at = pl.multiple_of(cycle * PANEL + partner * share, share)
        swaps.append((acc.at[pl.ds(at, share)], got_prod.at[cycle]))
    swaps.append((acc.at[pl.ds(top, 2 * PANEL)], got_gram))
    copies = []
    for k, (source, target) in enumerate(swaps):
        copies.append(pltpu.make_async_remote_copy(
            src_ref=source, dst_ref=target, send_sem=swap_sem.at[0, k], recv_sem=swap_sem.at[1, k],
            device_id=(row, partner), device_id_type=MESH))
    for copy in copies:
        copy.start()
    for s in range(2):
        for t in range(TREES):
            for way in range(4):
                wanted = sends[s][t][way]
                if wanted is None:
                    continue

                @pl.when(wanted)
                def _():
                    whole = piece(s, t, 0, counts[t])
                    pltpu.make_async_remote_copy(
                        src_ref=whole, dst_ref=whole,
                        send_sem=send_sem.at[s, t, way], recv_sem=recv_sem.at[s, t, 0],
                        device_id=(targets[way], col), device_id_type=MESH,
                    ).wait_send()
    for copy in copies:
        copy.wait()
    for cycle in range(cycles):
        at = pl.multiple_of(cycle * PANEL + col * share, share)
        prod_ref[cycle] = acc[pl.ds(at, share)] + got_prod[cycle]
    gram_ref[...] = acc[top:] + got_gram[...]


def on_device(rows, factor, scales, coords, jitter):
    cycles, block_rows, width_local = factor.shape
    lead_width = 2 * PANEL
    col_count = lax.axis_size("col")
    share_rows = PANEL // col_count
    chunks = width_local // CHUNK
    pieces, gram_sum = pl.pallas_call(
        functools.partial(gather_products, rows),
        out_shape=(
            jax.ShapeDtypeStruct((cycles, share_rows, lead_width), jnp.float32),
            jax.ShapeDtypeStruct((lead_width, lead_width), jnp.float32),
        ),
        in_specs=[
            pl.BlockSpec(memory_space=pl.ANY),
            pl.BlockSpec(memory_space=pltpu.SMEM),
        ],
        out_specs=(
            pl.BlockSpec(memory_space=pltpu.VMEM),
            pl.BlockSpec(memory_space=pltpu.VMEM),
        ),
        scratch_shapes=[
            pltpu.VMEM((cycles, PANEL, width_local), jnp.bfloat16),
            pltpu.VMEM((2, chunks, PANEL, CHUNK), jnp.bfloat16),
            pltpu.VMEM((cycles * PANEL, GROUP * CHUNK), jnp.bfloat16),
            pltpu.VMEM((cycles * PANEL + lead_width, lead_width), jnp.float32),
            pltpu.VMEM((cycles, share_rows, lead_width), jnp.float32),
            pltpu.VMEM((lead_width, lead_width), jnp.float32),
            pltpu.SemaphoreType.DMA((TREES, 2)),
            pltpu.SemaphoreType.DMA((2, TREES, 4)),
            pltpu.SemaphoreType.DMA((2, TREES, max(counts_of(chunks)))),
            pltpu.SemaphoreType.DMA((2, cycles + 1)),
        ],
        compiler_params=pltpu.CompilerParams(
            collective_id=0, has_side_effects=True, vmem_limit_bytes=48 * 1024 * 1024),
        cost_estimate=pl.CostEstimate(
            flops=8 * cycles * PANEL * lead_width * width_local,
            bytes_accessed=factor.size * 2, transcendentals=0),
        name="gather_products",
    )(factor, scales.reshape(cycles, -1))
    row_index = lax.axis_index("row")
    col_index = lax.axis_index("col")
    row_count = lax.axis_size("row")
    own_pts = lax.dynamic_slice_in_dim(
        coords, row_index * PANEL + col_index * share_rows, share_rows, 2
    ).reshape(2, cycles * share_rows)
    lead_pts = coords[:, 0, :lead_width]
    local_rows = jnp.arange(cycles * share_rows, dtype=jnp.int32)
    global_rows = (
        local_rows // share_rows * (row_count * PANEL)
        + row_index * PANEL + col_index * share_rows + local_rows % share_rows
    )
    identity_mask = (
        global_rows[:, None] == jnp.arange(lead_width, dtype=jnp.int32)[None, :]
    ).astype(jnp.float32)
    kernel = matern(own_pts, lead_pts) + jitter[0] * identity_mask
    lead_kernel = matern(lead_pts, lead_pts) + jitter[0] * jnp.eye(lead_width, dtype=jnp.float32)
    solved = pl.pallas_call(
        solve_panels,
        out_shape=jax.ShapeDtypeStruct((cycles * share_rows, lead_width), jnp.float32),
        scratch_shapes=[pltpu.VMEM((PANEL, PANEL), jnp.float32)] * 3,
        compiler_params=pltpu.CompilerParams(vmem_limit_bytes=16 * 1024 * 1024),
        name="solve_panels",
    )(gram_sum, lead_kernel, pieces.reshape(cycles * share_rows, lead_width), kernel)
    return solved.reshape(cycles, share_rows, lead_width)


def solution(mesh):
    placed = (P(None, "row", "col"), P(None, "row", "col"), P(), P())
    return jax.shard_map(
        functools.partial(on_device, mesh.shape["row"]),
        mesh=mesh,
        in_specs=placed,
        out_specs=P(None, ("row", "col"), None),
        check_vma=False,
    )
```

```python
import functools
import jax
import jax.numpy as jnp
from jax import lax
from jax.experimental import pallas as pl
from jax.experimental.pallas import tpu as pltpu
from jax.sharding import PartitionSpec as P

PANEL = 128
CHUNK = 128
GROUP = 4
SKEW = 3
HEAD = 8

SQRT_THREE = 1.7320508075688772
LENGTH_SCALE = 0.25
MESH = pl.DeviceIdType.MESH
TREES = 3
TWIN, CHAIN, LIFT = 0, 2, 1


def matern(left_pts, right_pts):
    diff_x = left_pts[0][:, None] - right_pts[0][None, :]
    diff_y = left_pts[1][:, None] - right_pts[1][None, :]
    scaled = SQRT_THREE * jnp.sqrt(diff_x * diff_x + diff_y * diff_y) / LENGTH_SCALE
    return (1.0 + scaled) * jnp.exp(-scaled)


def exact_dot(left, right, transposed):
    dims = (((1,), (1 if transposed else 0,)), ((), ()))
    return lax.dot_general(
        left, right, dims, precision=lax.Precision.HIGHEST, preferred_element_type=jnp.float32
    )


def inverse_factor(block, out_ref):
    size = block.shape[0]
    tiles = size // 8
    sub = lax.broadcasted_iota(jnp.int32, (8, size), 0)
    lane = lax.broadcasted_iota(jnp.int32, (8, size), 1)
    left = [block[8 * k:8 * k + 8] for k in range(tiles)]
    right = [(lane == sub + 8 * k).astype(jnp.float32) for k in range(tiles)]
    for j in range(0, size, 2):
        home, r = j // 8, j % 8
        left_one, left_two = left[home][r:r + 1, :], left[home][r + 1:r + 2, :]
        right_one, right_two = right[home][r:r + 1, :], right[home][r + 1:r + 2, :]
        first = jnp.broadcast_to(left_one[:, j:j + 1], (1, size))
        cross = jnp.broadcast_to(left_one[:, j + 1:j + 2], (1, size))
        second = jnp.broadcast_to(left_two[:, j + 1:j + 2], (1, size))
        det = first * second - cross * cross
        lower = first * right_two - cross * right_one
        out_ref[j:j + 1, :] = right_one * lax.rsqrt(first)
        out_ref[j + 1:j + 2, :] = lower * lax.rsqrt(first * det)
        if j + 2 == size:
            break
        inverse = 1.0 / det
        solved_left = (
            (second * left_one - cross * left_two) * inverse,
            (first * left_two - cross * left_one) * inverse,
        )
        solved_right = (
            (second * right_one - cross * right_two) * inverse,
            lower * inverse,
        )
        for k in range(home, tiles):
            if k == home and r == 6:
                continue
            columns = [jnp.broadcast_to(left[k][:, j + m:j + m + 1], (8, size)) for m in range(2)]
            if k == home:
                columns = [jnp.where(sub > r + 1, column, 0.0) for column in columns]
            left[k] = left[k] - (columns[0] * solved_left[0] + columns[1] * solved_left[1])
            right[k] = right[k] - (columns[0] * solved_right[0] + columns[1] * solved_right[1])


def solve_panels(gram_ref, lead_ref, prod_ref, kernel_ref, out_ref, block, inv_one, inv_two):
    half = block.shape[0]
    block[...] = lead_ref[:half, :half] - gram_ref[:half, :half]
    inverse_factor(block[...], inv_one)
    first = inv_one[...]
    below = exact_dot(lead_ref[half:, :half] - gram_ref[half:, :half], first, True)
    block[...] = lead_ref[half:, half:] - gram_ref[half:, half:] - exact_dot(below, below, True)
    one = exact_dot(kernel_ref[:, :half] - prod_ref[:, :half], first, True)
    rest = kernel_ref[:, half:] - prod_ref[:, half:] - exact_dot(one, below, True)
    inverse_factor(block[...], inv_two)
    out_ref[:, :half] = one
    out_ref[:, half:] = exact_dot(rest, inv_two[...], True)


def counts_of(chunks):
    groups = chunks // GROUP
    return [GROUP * (groups // TREES + (1 if t < groups % TREES else 0)) for t in range(TREES)]


def roles(tree, xs, y, z, planes):
    top = z == planes - 1
    low = z == 0
    a = (xs == 0) & (y == 0)
    b = (xs == 1) & (y == 0)
    c = (xs == 1) & (y == 1)
    d = (xs == 0) & (y == 1)
    up = jnp.logical_not(top)
    if tree == TWIN:
        return z + y + xs, xs == 0, a & low, (xs == 0) & up, None
    high = jnp.logical_not(low)
    if tree == CHAIN:
        depth = jnp.where(low, xs + y, z + jnp.where(d, 1, jnp.where(b, 3, 2)))
        send_x = (low & (xs == 0)) | (high & d)
        send_y = (low & a) | (high & (d | c))
        return depth, send_x, send_y, d & up, None
    place = jnp.where(a, 0, jnp.where(c, 2, 1))
    depth = jnp.where(low, jnp.where(a, 0, place + 2), z + place)
    return depth, high & a, high & (a | b), a & up, (z == 1) & jnp.logical_not(a)


def gather_products(rows, factor_hbm, scales_ref, prod_ref, gram_ref,
                    raw, lead, lhs, acc, got_prod, got_gram,
                    load_sem, send_sem, recv_sem, swap_sem):
    cycles, _, width = raw.shape
    row = lax.axis_index("row")
    col = lax.axis_index("col")
    chunks = width // CHUNK
    counts = counts_of(chunks)
    starts = [sum(counts[:t]) for t in range(TREES)]
    planes = rows // 4
    x = row % 2
    y = (row // 2) % 2
    z = row // 4
    targets = [
        row + 1 - 2 * x,
        row + 2 - 4 * y,
        jnp.minimum(row + 4, rows - 1),
        jnp.maximum(row - 4, 0),
    ]
    has_up = z < planes - 1
    has_down = z > 0
    partner = 1 - col

    head = min(HEAD, min(counts) - GROUP)
    loads = []
    for t in range(TREES):
        for part, (low, size) in enumerate(((0, head), (head, counts[t] - head))):
            span = pl.ds((starts[t] + low) * CHUNK, size * CHUNK)
            loads.append(pltpu.make_async_copy(
                factor_hbm.at[:, :, span], raw.at[:, :, span], load_sem.at[t, part]))
    for t in range(TREES):
        loads[2 * t].start()
    for t in range(TREES):
        loads[2 * t + 1].start()

    barrier = pltpu.get_barrier_semaphore()

    def greet(target):
        pl.semaphore_signal(barrier, inc=1, device_id=target, device_id_type=MESH)

    greet((targets[0], col))
    greet((targets[1], col))
    greet((row, partner))
    pl.when(has_up)(lambda: greet((targets[2], col)))
    pl.when(has_down)(lambda: greet((targets[3], col)))
    acc[...] = jnp.zeros_like(acc)
    pl.semaphore_wait(barrier, 3 + has_up.astype(jnp.int32) + has_down.astype(jnp.int32))

    depths = [[None] * TREES for _ in range(2)]
    sends = [[None] * TREES for _ in range(2)]
    for s in range(2):
        xs = x if s == 0 else 1 - x
        for t in range(TREES):
            depth, *send = roles(t, xs, y, z, planes)
            depths[s][t] = depth
            sends[s][t] = send
    deepest = [planes + 1, planes + 1, planes + 2]
    delays = [0, 1, 0]
    steps = max(counts[t] + SKEW * deepest[t] + delays[t] for t in range(TREES))

    def piece(s, t, index, size=1):
        return lead.at[s, pl.ds(starts[t] + index, size)]

    def dequantize(cycle, chunk):
        at = pl.multiple_of(chunk * CHUNK, CHUNK)
        block = raw[cycle, :, pl.ds(at, CHUNK)].astype(jnp.float32) * scales_ref[cycle, chunk]
        return block.astype(jnp.bfloat16)

    def forward(s, t, step):
        index = step - SKEW * depths[s][t]

        @pl.when((index >= 0) & (index < counts[t]))
        def _():
            here = piece(s, t, index)

            @pl.when(row == s)
            def _():
                lead[s, starts[t] + index] = dequantize(0, starts[t] + index)

            @pl.when(row != s)
            def _():
                pltpu.make_async_copy(here, here, recv_sem.at[s, t, index]).wait()

            for way in (2, 3, 0, 1):
                wanted = sends[s][t][way]
                if wanted is None:
                    continue

                @pl.when(wanted)
                def _():
                    pltpu.make_async_remote_copy(
                        src_ref=here, dst_ref=here,
                        send_sem=send_sem.at[s, t, way], recv_sem=recv_sem.at[s, t, index],
                        device_id=(targets[way], col), device_id_type=MESH,
                    ).start()

    def multiply(t, step):
        index = step - SKEW * jnp.maximum(depths[0][t], depths[1][t]) - delays[t]

        @pl.when((index >= 0) & (index < counts[t]) & (index % GROUP == GROUP - 1))
        def _():
            first = starts[t] + index - (GROUP - 1)
            for cycle in range(cycles):
                for b in range(GROUP):
                    lhs[cycle * PANEL:(cycle + 1) * PANEL, b * CHUNK:(b + 1) * CHUNK] = (
                        dequantize(cycle, first + b))
            right = jnp.concatenate([
                jnp.concatenate([lead[s, first + b] for b in range(GROUP)], axis=1)
                for s in range(2)], axis=0)
            dims = (((1,), (1,)), ((), ()))
            own = jnp.concatenate([lhs[...], right], axis=0)
            acc[...] += lax.dot_general(own, right, dims, preferred_element_type=jnp.float32)

    def one_step(step, carry):
        for t in (CHAIN, LIFT, TWIN):
            for s in range(2):
                forward(s, t, step)
        for t in range(TREES):
            multiply(t, step)
        return carry

    for t in range(TREES):
        loads[2 * t].wait()
    lax.fori_loop(0, head, one_step, 0)
    for t in range(TREES):
        loads[2 * t + 1].wait()
    lax.fori_loop(head, steps, one_step, 0)

    share = PANEL // 2
    top = cycles * PANEL
    swaps = []
    for cycle in range(cycles):
        at = pl.multiple_of(cycle * PANEL + partner * share, share)
        swaps.append((acc.at[pl.ds(at, share)], got_prod.at[cycle]))
    swaps.append((acc.at[pl.ds(top, 2 * PANEL)], got_gram))
    copies = []
    for k, (source, target) in enumerate(swaps):
        copies.append(pltpu.make_async_remote_copy(
            src_ref=source, dst_ref=target, send_sem=swap_sem.at[0, k], recv_sem=swap_sem.at[1, k],
            device_id=(row, partner), device_id_type=MESH))
    for copy in copies:
        copy.start()
    for s in range(2):
        for t in range(TREES):
            for way in range(4):
                wanted = sends[s][t][way]
                if wanted is None:
                    continue

                @pl.when(wanted)
                def _():
                    whole = piece(s, t, 0, counts[t])
                    pltpu.make_async_remote_copy(
                        src_ref=whole, dst_ref=whole,
                        send_sem=send_sem.at[s, t, way], recv_sem=recv_sem.at[s, t, 0],
                        device_id=(targets[way], col), device_id_type=MESH,
                    ).wait_send()
    for copy in copies:
        copy.wait()
    for cycle in range(cycles):
        at = pl.multiple_of(cycle * PANEL + col * share, share)
        prod_ref[cycle] = acc[pl.ds(at, share)] + got_prod[cycle]
    gram_ref[...] = acc[top:] + got_gram[...]


def on_device(rows, factor, scales, coords, jitter):
    cycles, block_rows, width_local = factor.shape
    lead_width = 2 * PANEL
    col_count = lax.axis_size("col")
    share_rows = PANEL // col_count
    chunks = width_local // CHUNK
    pieces, gram_sum = pl.pallas_call(
        functools.partial(gather_products, rows),
        out_shape=(
            jax.ShapeDtypeStruct((cycles, share_rows, lead_width), jnp.float32),
            jax.ShapeDtypeStruct((lead_width, lead_width), jnp.float32),
        ),
        in_specs=[
            pl.BlockSpec(memory_space=pl.ANY),
            pl.BlockSpec(memory_space=pltpu.SMEM),
        ],
        out_specs=(
            pl.BlockSpec(memory_space=pltpu.VMEM),
            pl.BlockSpec(memory_space=pltpu.VMEM),
        ),
        scratch_shapes=[
            pltpu.VMEM((cycles, PANEL, width_local), jnp.bfloat16),
            pltpu.VMEM((2, chunks, PANEL, CHUNK), jnp.bfloat16),
            pltpu.VMEM((cycles * PANEL, GROUP * CHUNK), jnp.bfloat16),
            pltpu.VMEM((cycles * PANEL + lead_width, lead_width), jnp.float32),
            pltpu.VMEM((cycles, share_rows, lead_width), jnp.float32),
            pltpu.VMEM((lead_width, lead_width), jnp.float32),
            pltpu.SemaphoreType.DMA((TREES, 2)),
            pltpu.SemaphoreType.DMA((2, TREES, 4)),
            pltpu.SemaphoreType.DMA((2, TREES, max(counts_of(chunks)))),
            pltpu.SemaphoreType.DMA((2, cycles + 1)),
        ],
        compiler_params=pltpu.CompilerParams(
            collective_id=0, has_side_effects=True, vmem_limit_bytes=48 * 1024 * 1024),
        cost_estimate=pl.CostEstimate(
            flops=8 * cycles * PANEL * lead_width * width_local,
            bytes_accessed=factor.size * 2, transcendentals=0),
        name="gather_products",
    )(factor, scales.reshape(cycles, -1))
    row_index = lax.axis_index("row")
    col_index = lax.axis_index("col")
    row_count = lax.axis_size("row")
    own_pts = lax.dynamic_slice_in_dim(
        coords, row_index * PANEL + col_index * share_rows, share_rows, 2
    ).reshape(2, cycles * share_rows)
    lead_pts = coords[:, 0, :lead_width]
    local_rows = jnp.arange(cycles * share_rows, dtype=jnp.int32)
    global_rows = (
        local_rows // share_rows * (row_count * PANEL)
        + row_index * PANEL + col_index * share_rows + local_rows % share_rows
    )
    identity_mask = (
        global_rows[:, None] == jnp.arange(lead_width, dtype=jnp.int32)[None, :]
    ).astype(jnp.float32)
    kernel = matern(own_pts, lead_pts) + jitter[0] * identity_mask
    lead_kernel = matern(lead_pts, lead_pts) + jitter[0] * jnp.eye(lead_width, dtype=jnp.float32)
    solved = pl.pallas_call(
        solve_panels,
        out_shape=jax.ShapeDtypeStruct((cycles * share_rows, lead_width), jnp.float32),
        scratch_shapes=[pltpu.VMEM((PANEL, PANEL), jnp.float32)] * 3,
        compiler_params=pltpu.CompilerParams(vmem_limit_bytes=16 * 1024 * 1024),
        name="solve_panels",
    )(gram_sum, lead_kernel, pieces.reshape(cycles * share_rows, lead_width), kernel)
    return solved.reshape(cycles, share_rows, lead_width)


def solution(mesh):
    placed = (P(None, "row", "col"), P(None, "row", "col"), P(), P())
    return jax.shard_map(
        functools.partial(on_device, mesh.shape["row"]),
        mesh=mesh,
        in_specs=placed,
        out_specs=P(None, ("row", "col"), None),
        check_vma=False,
    )
```
